32 devices in a mesh: view: 4 (over y, x), joined: 8 (over z, core).
Axes of the slice: x: 2, y: 2, z: 4, core: 2. Of those that a mesh axis runs over, the one named last changes fastest.
Arguments:
- observed: float32 [4, 256, 16, 16, 128], P('view', 'joined'), may hold values from 0.25 to 4
- estimate: float32 [256, 16, 16, 128], P('joined'), may hold values from 0.5 to 2
- psf_taps: float32 [4, 3, 31], P('view'), may hold values from 0.02 to 1
- tile_block: int32 [4, 256], replicated, may hold values from 0 to 255, as said below
- weight_level: int32 [4, 256], P('view', 'joined'), may hold values from 0 to 7
Outputs:
- refined: float32 [256, 16, 16, 128], P('joined')
The draws below stay inside these ranges and needn't reach their ends.
Inputs may be any that keep to these rules, and one draw needn't show every extreme that they name: `tile_block`: for each view the list names every one of the 256 blocks exactly once. Block b belongs to index b // 32 of joined; the tiles of one device are the aligned runs of 32 entries. Of one device's tiles of one view at most 8 lie in blocks of one owner, and in every view each device has an owner that gets exactly 8 of them.
All inputs are finite; a program needn't handle non-finite values.
Results may differ from the reference program's by a relative error of at most 0.0001.
Values sent between devices are 32-bit elements; how exact they have to be, the bound alone decides.
A program may use at most 128 MiB of HBM per device.

```python
import math
import jax
import jax.numpy as jnp
from jax import lax

BZ = 16
BY = 16
BX = 128
TILE_DEV = 32
TAPS = 31
ITERS = 1
VIEWS = 4
TILES = 256
CAP = 8


def draw_tile_block(key, part):
    key = jax.random.fold_in(key, 11)
    owner_count = TILES // TILE_DEV

    def one_view(view_key):
        key_load, key_label, key_owner, key_tile, key_block = jax.random.split(view_key, 5)
        pair_count = owner_count // 2
        first_load = jax.random.randint(key_load, (pair_count,), 0, CAP + 1).at[0].set(CAP)
        loads = jnp.stack([first_load, CAP - first_load], axis=1).reshape(owner_count)
        run_ends = jnp.cumsum(loads)
        item_ids = jnp.arange(TILE_DEV)
        run_index = jnp.sum((run_ends[None, :] <= item_ids[:, None]).astype(jnp.int32), axis=1)
        labels = jax.random.permutation(key_label, owner_count)
        shift_list = labels[run_index]
        relabel = jax.random.permutation(key_owner, owner_count)
        devices = jnp.arange(owner_count)
        owner_of = relabel[(devices[:, None] + shift_list[None, :]) % owner_count]
        tile_perm = jax.vmap(lambda part_key: jax.random.permutation(part_key, TILE_DEV))(jax.random.split(key_tile, owner_count))
        block_perm = jax.vmap(lambda part_key: jax.random.permutation(part_key, TILE_DEV))(jax.random.split(key_block, owner_count))
        block_of = owner_of * TILE_DEV + block_perm[owner_of, item_ids[None, :]]
        placed = devices[:, None] * TILE_DEV + tile_perm
        return jnp.zeros((TILES,), jnp.int32).at[placed.reshape(-1)].set(block_of.reshape(-1).astype(jnp.int32))
    return jax.vmap(one_view)(jax.random.split(key, VIEWS))


def draw_estimate(key, part):
    key = jax.random.fold_in(key, 37)
    key_pick, key_low, key_high = jax.random.split(key, 3)
    shape_all = (TILES, BZ, BY, BX)
    upper = jax.random.uniform(key_pick, shape_all, jnp.float32) < 0.5
    lower_vals = jax.random.uniform(key_low, shape_all, jnp.float32, 0.5, 0.8)
    upper_vals = jax.random.uniform(key_high, shape_all, jnp.float32, 1.4, 2.0)
    return jnp.where(upper, upper_vals, lower_vals).astype(jnp.float32)


def draw_psf_taps(key, part):
    key = jax.random.fold_in(key, 23)
    key_side, key_peak = jax.random.split(key, 2)
    sides = jnp.exp(jax.random.uniform(key_side, (VIEWS, 3, TAPS), jnp.float32, jnp.log(0.02), jnp.log(0.04)))
    peaks = jax.random.uniform(key_peak, (VIEWS, 3, 1), jnp.float32, 0.8, 1.0)
    centre = (jnp.arange(TAPS) == TAPS // 2)[None, None, :]
    return jnp.where(centre, peaks, sides).astype(jnp.float32)


def with_ends(drawn, stream_key, smallest, largest):
    shape = drawn.shape
    spot = [jax.random.randint(jax.random.fold_in(stream_key, axis), (), 0, shape[axis]) for axis in range(len(shape))]
    drawn = drawn.at[tuple(spot)].set(smallest)
    longest = shape.index(max(shape))
    spot[longest] = (spot[longest] + 1) % shape[longest]
    return drawn.at[tuple(spot)].set(largest)


def level_of(stream_key, shape, pieces, smallest, top_value):
    level, own = 1.0, jax.random.fold_in(stream_key, 6)
    for position, blocks in pieces:
        steps = jnp.exp(jax.random.uniform(jax.random.fold_in(own, position), (blocks,), jnp.float32, smallest / len(pieces), top_value / len(pieces)))
        level = level * jnp.repeat(steps, shape[position] // blocks).reshape([-1 if axis == position else 1 for axis in range(len(shape))])
    return level


def setup_inputs(seed: int = 0) -> dict:
    splits = jax.random.split(jax.random.key(seed), 6)
    return {
        "observed": jnp.clip(jnp.exp(math.log(4.0) - 2.7725887 * jax.random.uniform(splits[0], (VIEWS, TILES, BZ, BY, BX), jnp.float32) ** level_of(splits[0], (VIEWS, TILES, BZ, BY, BX), ((0, 4), (1, 8)), -0.2, 0.2)), 0.25, 4.0),
        "estimate": draw_estimate(jax.random.fold_in(splits[5], 71), 0),
        "psf_taps": draw_psf_taps(jax.random.fold_in(splits[5], 71), 0),
        "tile_block": draw_tile_block(jax.random.fold_in(splits[5], 71), 0),
        "weight_level": with_ends(jax.random.randint(splits[4], (VIEWS, TILES), 0, 8), jax.random.fold_in(splits[4], 1), 0, 7).astype(jnp.int32),
    }


def band(kernel_row, extent):
    half_span = kernel_row.shape[0] // 2
    offset = jnp.arange(extent)[None, :] - jnp.arange(extent)[:, None] + half_span
    chosen = (offset[:, :, None] == jnp.arange(kernel_row.shape[0])[None, None, :]).astype(jnp.float32)
    return jnp.sum(chosen * kernel_row[None, None, :], axis=-1)


def shifted(volume, kernel_row, flipped):
    tap_count = kernel_row.shape[0]
    half_span = tap_count // 2
    extent_x = volume.shape[3]
    padded = jnp.pad(volume, ((0, 0), (0, 0), (0, 0), (half_span, half_span)))
    summed = jnp.zeros_like(volume)
    for tap_index in range(tap_count):
        begin = 2 * half_span - tap_index if flipped else tap_index
        summed = summed + kernel_row[tap_index] * padded[:, :, :, begin:begin + extent_x]
    return summed


def blur(volume, kernel_set):
    along_z = band(kernel_set[0], volume.shape[1])
    along_y = band(kernel_set[1], volume.shape[2])
    volume = jnp.einsum("az,tzyx->tayx", along_z, volume, precision=lax.Precision.HIGHEST)
    volume = jnp.einsum("by,tzyx->tzbx", along_y, volume, precision=lax.Precision.HIGHEST)
    return shifted(volume, kernel_set[2], False)


def spread(volume, kernel_set):
    along_z = band(kernel_set[0], volume.shape[1])
    along_y = band(kernel_set[1], volume.shape[2])
    volume = shifted(volume, kernel_set[2], True)
    volume = jnp.einsum("yb,tzyx->tzbx", along_y, volume, precision=lax.Precision.HIGHEST)
    return jnp.einsum("za,tzyx->tayx", along_z, volume, precision=lax.Precision.HIGHEST)


def reference(observed, estimate, psf_taps, tile_block, weight_level):
    kernel = psf_taps / jnp.sum(psf_taps, axis=-1, keepdims=True)
    weights = (weight_level.astype(jnp.float32) + 1.0) / 8.0
    current = estimate
    for sweep in range(ITERS):
        numerator = jnp.zeros_like(current)
        denominator = jnp.zeros((current.shape[0],), jnp.float32)
        for view_index in range(VIEWS):
            block_list = tile_block[view_index].astype(jnp.int32)
            blurred = blur(current[block_list], kernel[view_index])
            ratio_field = observed[view_index] / blurred
            spread_back = spread(ratio_field, kernel[view_index])
            numerator = numerator.at[block_list].add(weights[view_index][:, None, None, None] * spread_back)
            denominator = denominator.at[block_list].add(weights[view_index])
        current = current * (numerator / denominator[:, None, None, None])
    return current
```

```python
import functools

import jax
import jax.numpy as jnp
from jax import lax
from jax.experimental import pallas as pl
from jax.experimental.pallas import tpu as pltpu
from jax.sharding import PartitionSpec as P


def bands(rows, extent):
    taps = rows.shape[-1]
    offset = jnp.arange(extent)[None, :] - jnp.arange(extent)[:, None] + taps // 2
    chosen = (offset[:, :, None] == jnp.arange(taps)[None, None, :]).astype(jnp.float32)
    return jnp.sum(chosen * rows, axis=-1)


def split(value):
    high = value.astype(jnp.bfloat16)
    low = (value - high.astype(jnp.float32)).astype(jnp.bfloat16)
    return high, low


def matmul(a, b):
    dot = functools.partial(jnp.dot, preferred_element_type=jnp.float32)
    return dot(a[0], b[0]) + (dot(a[0], b[1]) + dot(a[1], b[0]))


def project_kernel(slot_ref, plane_ref, back_ref, line_ref, lineback_ref, weight_ref, seen_ref, estimate_ref, out_ref):
    block = pl.program_id(0)
    current = estimate_ref[0]
    blurred = matmul(split(matmul(split(plane_ref[...]), split(current))), split(lineback_ref[...]))
    ratio = seen_ref[0] / blurred
    spread = matmul(split(matmul(split(back_ref[...]), split(ratio))), split(line_ref[...]))
    out_ref[0] = weight_ref[block] * spread


def project(slot, plane, line, weight, seen, estimate):
    blocks, rows, lanes = estimate.shape
    whole = lambda array: pl.BlockSpec(array.shape, lambda i, slot: (0,) * array.ndim)
    return pl.pallas_call(
        project_kernel,
        grid_spec=pltpu.PrefetchScalarGridSpec(
            num_scalar_prefetch=1,
            grid=(blocks,),
            in_specs=[
                whole(plane),
                whole(plane),
                whole(line),
                whole(line),
                pl.BlockSpec(memory_space=pltpu.SMEM),
                pl.BlockSpec((1, rows, lanes), lambda i, slot: (slot[i], 0, 0)),
                pl.BlockSpec((1, rows, lanes), lambda i, slot: (i, 0, 0)),
            ],
            out_specs=pl.BlockSpec((1, rows, lanes), lambda i, slot: (i, 0, 0)),
        ),
        out_shape=jax.ShapeDtypeStruct(estimate.shape, jnp.float32),
        compiler_params=pltpu.CompilerParams(vmem_limit_bytes=32 * 1024 * 1024),
    )(slot, plane, plane.T, line, line.T, weight, seen, estimate)


def shards(observed, estimate, psf_taps, tile_block, weight_level):
    owner_count = lax.axis_size("joined")
    view_here, joined_here = lax.axis_index("view"), lax.axis_index("joined")
    tiles_dev, size_z, size_y, size_x = estimate.shape
    rows = size_z * size_y
    slot_count = 2 * tiles_dev // owner_count
    all_slots = owner_count * slot_count

    kernel_rows = psf_taps[0] / jnp.sum(psf_taps[0], axis=-1, keepdims=True)
    along_z = bands(kernel_rows[0], size_z)
    along_y = bands(kernel_rows[1], size_y)
    line = bands(kernel_rows[2], size_x)
    plane = (along_z[:, None, :, None] * along_y[None, :, None, :]).reshape(rows, rows)

    listing = lax.dynamic_index_in_dim(tile_block, view_here, 0, keepdims=False)
    owners = (listing // tiles_dev).reshape(owner_count, tiles_dev)
    earlier = jnp.arange(tiles_dev)[None, :] < jnp.arange(tiles_dev)[:, None]
    matching = owners[:, :, None] == owners[:, None, :]
    rank = jnp.sum((matching & earlier[None]).astype(jnp.int32), axis=2)
    source = jnp.arange(owner_count, dtype=jnp.int32)[:, None]
    arrive = (source * slot_count + rank).reshape(-1)
    here = lax.dynamic_slice_in_dim(owners * slot_count + rank, joined_here, 1, 0)[0]
    fills = here[None, :] == jnp.arange(all_slots)[:, None]
    outgoing = jnp.sum(fills * jnp.arange(tiles_dev)[None, :], axis=1)
    local = jnp.arange(tiles_dev, dtype=jnp.int32) + joined_here * tiles_dev
    hits = (listing[None, :] == local[:, None]).astype(jnp.int32)
    slot = jnp.sum(hits * arrive[None, :], axis=1)

    tile_weight = (weight_level[0].astype(jnp.float32) + 1.0) / 8.0
    all_weight = lax.all_gather(tile_weight, "joined", tiled=True)
    weight = jnp.sum(hits.astype(jnp.float32) * all_weight[None, :], axis=1)

    tiles = observed.reshape(tiles_dev, rows, size_x)
    packed = jnp.take(tiles, outgoing, axis=0, mode="clip")
    arrived = lax.all_to_all(
        packed.reshape(owner_count, slot_count, rows, size_x), "joined", 0, 0, tiled=True
    ).reshape(all_slots, rows, size_x)
    current = estimate.reshape(tiles_dev, rows, size_x)
    part = project(slot, plane, line, weight, arrived, current)
    numerator, denominator = lax.psum((part, weight), "view")
    refined = current * (numerator / denominator[:, None, None])
    return refined.reshape(estimate.shape)


def solution(mesh):
    return jax.shard_map(
        shards,
        mesh=mesh,
        in_specs=(
            P("view", "joined", None, None, None),
            P("joined", None, None, None),
            P("view", None, None),
            P(),
            P("view", "joined"),
        ),
        out_specs=P("joined", None, None, None),
        check_vma=False,
    )
```

```python
import functools

import jax
import jax.numpy as jnp
from jax import lax
from jax.experimental import pallas as pl
from jax.experimental.pallas import tpu as pltpu
from jax.sharding import PartitionSpec as P

PARTS = (80, 80, 64, 32)
PIECES = len(PARTS)
STARTS = tuple(sum(PARTS[:p]) for p in range(PIECES))
MESH = pl.DeviceIdType.MESH


def bands(rows, extent):
    taps = rows.shape[-1]
    offset = jnp.arange(extent)[None, :] - jnp.arange(extent)[:, None] + taps // 2
    chosen = (offset[:, :, None] == jnp.arange(taps)[None, None, :]).astype(jnp.float32)
    return jnp.sum(chosen * rows, axis=-1)


def split(value):
    high = value.astype(jnp.bfloat16)
    low = (value - high.astype(jnp.float32)).astype(jnp.bfloat16)
    return high, low


def matmul(a, b):
    dot = functools.partial(jnp.dot, preferred_element_type=jnp.float32)
    return dot(a[0], b[0]) + (dot(a[0], b[1]) + dot(a[1], b[0]))


def kernel(
    views, owners, slots,
    outgoing, slot_weight, slot, planes, lines, seen, current, own_weight, out, weight_out, *scratch,
):
    sends, arrived, regroup = scratch[:PIECES], scratch[PIECES : 2 * PIECES], scratch[2 * PIECES : 3 * PIECES]
    (ratio_in, blurred, total, plane_all, line_all, plane_high, plane_low, line_high, line_low,
     z_send, z_recv, xy_send, xy_recv, m_send, m_recv, g_send, g_recv, own_sem,
     weight_all, w_send, w_recv, v_send, v_recv, w_sem) = scratch[3 * PIECES :]
    share, rows, lanes = current.shape
    here, view = lax.axis_index("joined"), lax.axis_index("view")
    owner_at = lambda d: lax.rem(here + d, owners)
    view_at = lambda u: lax.rem(view + u, views)
    sides = (view + 1 - 2 * lax.rem(view, 2), lax.rem(view + 2, 4))

    barrier = pltpu.get_barrier_semaphore()
    for d in range(1, owners):
        pl.semaphore_signal(barrier, inc=1, device_id={"joined": owner_at(d)}, device_id_type=MESH)
    for u in range(1, views):
        pl.semaphore_signal(barrier, inc=1, device_id={"view": view_at(u)}, device_id_type=MESH)
    pl.semaphore_wait(barrier, owners + views - 2)

    def matrix_copies(u):
        return [
            pltpu.make_async_remote_copy(
                src_ref=src, dst_ref=dst.at[view],
                send_sem=m_send.at[i, u - 1], recv_sem=m_recv.at[i, u - 1],
                device_id={"view": view_at(u)}, device_id_type=MESH,
            )
            for i, (src, dst) in enumerate(((planes, plane_all), (lines, line_all)))
        ]

    def z_copy(p, d):
        return pltpu.make_async_remote_copy(
            src_ref=sends[p].at[d - 1],
            dst_ref=arrived[p].at[pl.ds(here * slots, slots)],
            send_sem=z_send.at[p, d - 1], recv_sem=z_recv.at[p, d - 1],
            device_id={"joined": owner_at(d)}, device_id_type=MESH,
        )

    def xy_copy(p, u):
        return pltpu.make_async_remote_copy(
            src_ref=regroup[p].at[u - 1],
            dst_ref=ratio_in.at[view, :, pl.ds(STARTS[p], PARTS[p])],
            send_sem=xy_send.at[p, u - 1], recv_sem=xy_recv.at[p, u - 1],
            device_id={"view": view_at(u)}, device_id_type=MESH,
        )

    def gather_copy(k, side):
        return pltpu.make_async_remote_copy(
            src_ref=total.at[k], dst_ref=out.at[view, k],
            send_sem=g_send.at[k, side], recv_sem=g_recv.at[k, side],
            device_id={"view": sides[side]}, device_id_type=MESH,
        )

    def forward_copy(k, side):
        place = out.at[sides[side], k]
        return pltpu.make_async_remote_copy(
            src_ref=place, dst_ref=place,
            send_sem=g_send.at[k, 2], recv_sem=g_recv.at[k, 2],
            device_id={"view": sides[1 - side]}, device_id_type=MESH,
        )

    def weight_copy(d):
        return pltpu.make_async_remote_copy(
            src_ref=own_weight, dst_ref=weight_all.at[here],
            send_sem=w_send.at[d - 1], recv_sem=w_recv.at[d - 1],
            device_id={"joined": owner_at(d)}, device_id_type=MESH,
        )

    def weights_copy(u):
        return pltpu.make_async_remote_copy(
            src_ref=weight_all, dst_ref=weight_out.at[view],
            send_sem=v_send.at[u - 1], recv_sem=v_recv.at[u - 1],
            device_id={"view": view_at(u)}, device_id_type=MESH,
        )

    def own_copy(k):
        return pltpu.make_async_copy(total.at[k], out.at[view, k], own_sem.at[k])

    def pack(p):
        window = pl.ds(STARTS[p], PARTS[p])
        for d in list(range(1, owners)) + [0]:

            def fill(s, carry):
                at = owner_at(d) * slots + s
                piece = seen[outgoing[at], window] * slot_weight[at]
                if d == 0:
                    arrived[p][here * slots + s] = piece
                else:
                    sends[p][d - 1, s] = piece
                return carry

            lax.fori_loop(0, slots, fill, 0)
            if d:
                z_copy(p, d).start()

    def regroup_piece(p):
        for d in range(1, owners):
            z_copy(p, d).wait_recv()
        for u in list(range(1, views)) + [0]:

            def move(k, carry):
                piece = arrived[p][slot[view_at(u) * share + k]]
                if u == 0:
                    ratio_in[view, k, pl.ds(STARTS[p], PARTS[p])] = piece
                else:
                    regroup[p][u - 1, k] = piece
                return carry

            lax.fori_loop(0, share, move, 0)
            if u:
                xy_copy(p, u).start()

    own_weights = pltpu.make_async_copy(weight_all, weight_out.at[view], w_sem)
    pack(0)
    weight_all[here] = own_weight[...]
    for d in range(1, owners):
        weight_copy(d).start()
    plane_all[view] = planes[...]
    line_all[view] = lines[...]
    for u in range(1, views):
        for copy in matrix_copies(u):
            copy.start()
    pack(1)
    for u in range(1, views):
        for copy in matrix_copies(u):
            copy.wait_recv()

    def prepare(v, carry):
        for i in range(2):
            plane_high[v, i], plane_low[v, i] = split(plane_all[v, i])
            line_high[v, i], line_low[v, i] = split(line_all[v, i])

        def blur_one(k, inner):
            half = matmul(split(current[k]), (line_high[v, 1], line_low[v, 1]))
            blurred[v, k] = matmul((plane_high[v, 0], plane_low[v, 0]), split(half))
            return inner

        return lax.fori_loop(0, share, blur_one, carry)

    lax.fori_loop(0, views, prepare, 0)

    for p in range(PIECES):
        regroup_piece(p)
        if p == 0:
            for d in range(1, owners):
                weight_copy(d).wait_recv()
            for u in range(1, views):
                weights_copy(u).start()
            own_weights.start()
        if p + 2 < PIECES:
            pack(p + 2)
    for p in range(PIECES):
        for u in range(1, views):
            xy_copy(p, u).wait_recv()

    def finish_one(k):
        def back(v, inner):
            ratio = ratio_in[v, k] / blurred[v, k]
            half = matmul(split(ratio), (line_high[v, 0], line_low[v, 0]))
            return inner + matmul((plane_high[v, 1], plane_low[v, 1]), split(half))

        total[k] = lax.fori_loop(0, views, back, jnp.zeros((rows, lanes), jnp.float32))
        for side in range(2):
            gather_copy(k, side).start()
        own_copy(k).start()

    def forward_pair(pair):
        for side in range(2):
            gather_copy(2 * pair + side, side).wait_recv()
            forward_copy(2 * pair + side, side).start()

    def finish(pair, carry):
        finish_one(2 * pair)
        finish_one(2 * pair + 1)

        @pl.when(pair > 0)
        def _():
            forward_pair(pair - 1)

        return carry

    lax.fori_loop(0, share // 2, finish, 0)
    forward_pair(share // 2 - 1)

    for u in range(1, views):
        for copy in matrix_copies(u):
            copy.wait_send()
    for p in range(PIECES):
        for d in range(1, owners):
            z_copy(p, d).wait_send()
        for u in range(1, views):
            xy_copy(p, u).wait_send()

    for d in range(1, owners):
        weight_copy(d).wait_send()
    for u in range(1, views):
        weights_copy(u).wait()
    own_weights.wait()

    def drain(pair, carry):
        for side in range(2):
            k = 2 * pair + side
            own_copy(k).wait()
            gather_copy(k, side).wait_send()
            gather_copy(k, 1 - side).wait()
            forward_copy(k, side).wait()
        return carry

    lax.fori_loop(0, share // 2, drain, 0)


def exchange(views, owners, slots, outgoing, slot_weight, slot, planes, lines, seen, current, weight):
    share, rows, lanes = current.shape
    f32, bf16 = jnp.float32, jnp.bfloat16
    dma = pltpu.SemaphoreType.DMA
    smem, vmem = pl.BlockSpec(memory_space=pltpu.SMEM), pl.BlockSpec(memory_space=pltpu.VMEM)
    scratch = (
        [pltpu.VMEM((owners - 1, slots, part, lanes), f32) for part in PARTS]
        + [pltpu.VMEM((owners * slots, part, lanes), f32) for part in PARTS]
        + [pltpu.VMEM((views - 1, share, part, lanes), f32) for part in PARTS]
        + [pltpu.VMEM((views, share, rows, lanes), f32)] * 2
        + [pltpu.VMEM((share, rows, lanes), f32)]
        + [pltpu.VMEM((views,) + planes.shape, f32), pltpu.VMEM((views,) + lines.shape, f32)]
        + [pltpu.VMEM((views,) + planes.shape, bf16)] * 2
        + [pltpu.VMEM((views,) + lines.shape, bf16)] * 2
        + [dma((PIECES, owners - 1))] * 2
        + [dma((PIECES, views - 1))] * 2
        + [dma((2, views - 1))] * 2
        + [dma((share, 3))] * 2
        + [dma((share,))]
        + [pltpu.VMEM((owners,) + weight.shape, f32)]
        + [dma((owners - 1,))] * 2
        + [dma((views - 1,))] * 2
        + [dma(())]
    )
    return pl.pallas_call(
        functools.partial(kernel, views, owners, slots),
        out_shape=(
            jax.ShapeDtypeStruct((views, share, rows, lanes), f32),
            jax.ShapeDtypeStruct((views, owners) + weight.shape, f32),
        ),
        in_specs=[smem] * 3 + [vmem] * 5,
        out_specs=[pl.BlockSpec(memory_space=pl.ANY)] * 2,
        scratch_shapes=scratch,
        compiler_params=pltpu.CompilerParams(
            collective_id=0, has_side_effects=True, vmem_limit_bytes=56 * 1024 * 1024
        ),
        cost_estimate=pl.CostEstimate(
            flops=6 * 2 * views * share * 2 * rows * lanes * (rows + lanes) // 2,
            bytes_accessed=4 * (seen.size + 5 * current.size),
            transcendentals=0,
        ),
    )(outgoing, slot_weight, slot, planes, lines, seen, current, weight)


def shards(observed, estimate, psf_taps, tile_block, weight_level):
    owners, views = lax.axis_size("joined"), lax.axis_size("view")
    view_here, joined_here = lax.axis_index("view"), lax.axis_index("joined")
    tiles_dev, size_z, size_y, size_x = estimate.shape
    rows = size_z * size_y
    slots = 2 * tiles_dev // owners
    all_slots = owners * slots
    share = tiles_dev // views

    kernel_rows = psf_taps[0] / jnp.sum(psf_taps[0], axis=-1, keepdims=True)
    along_z = bands(kernel_rows[0], size_z)
    along_y = bands(kernel_rows[1], size_y)
    line = bands(kernel_rows[2], size_x)
    plane = (along_z[:, None, :, None] * along_y[None, :, None, :]).reshape(rows, rows)

    listing = lax.dynamic_index_in_dim(tile_block, view_here, 0, keepdims=False)
    owner_of = (listing // tiles_dev).reshape(owners, tiles_dev)
    earlier = jnp.arange(tiles_dev)[None, :] < jnp.arange(tiles_dev)[:, None]
    matching = owner_of[:, :, None] == owner_of[:, None, :]
    rank = jnp.sum((matching & earlier[None]).astype(jnp.int32), axis=2)
    source = jnp.arange(owners, dtype=jnp.int32)[:, None]
    arrive = (source * slots + rank).reshape(-1)
    here = lax.dynamic_slice_in_dim(owner_of * slots + rank, joined_here, 1, 0)[0]
    fills = (here[None, :] == jnp.arange(all_slots)[:, None]).astype(jnp.int32)
    outgoing = jnp.sum(fills * jnp.arange(tiles_dev, dtype=jnp.int32)[None, :], axis=1)
    local = jnp.arange(tiles_dev, dtype=jnp.int32) + joined_here * tiles_dev
    hits = (tile_block[:, None, :] == local[None, :, None]).astype(jnp.int32)
    hits_here = lax.dynamic_index_in_dim(hits, view_here, 0, keepdims=False)
    slot = jnp.sum(hits_here * arrive[None, :], axis=1)

    tile_weight = (weight_level[0].astype(jnp.float32) + 1.0) / 8.0
    slot_weight = jnp.sum(fills.astype(jnp.float32) * tile_weight[None, :], axis=1)
    current = estimate.reshape(tiles_dev, rows, size_x)
    mine = lax.dynamic_slice_in_dim(current, view_here * share, share, 0)
    weight_row = jnp.broadcast_to(jnp.pad(tile_weight, (0, -tiles_dev % 128)), (8, 128))
    numerator, all_weight = exchange(
        views, owners, slots,
        outgoing, slot_weight, slot,
        jnp.stack([plane, plane.T]), jnp.stack([line, line.T]),
        observed.reshape(tiles_dev, rows, size_x), mine, weight_row,
    )
    numerator = numerator.reshape(tiles_dev, rows, size_x)
    all_weight = all_weight[:, :, 0, :tiles_dev].reshape(views, 1, -1)
    denominator = jnp.sum(hits.astype(jnp.float32) * all_weight, axis=(0, 2))
    refined = current * (numerator / denominator[:, None, None])
    return refined.reshape(estimate.shape)


def solution(mesh):
    return jax.shard_map(
        shards,
        mesh=mesh,
        in_specs=(
            P("view", "joined", None, None, None),
            P("joined", None, None, None),
            P("view", None, None),
            P(),
            P("view", "joined"),
        ),
        out_specs=P("joined", None, None, None),
        check_vma=False,
    )
```

```python
import functools

import jax
import jax.numpy as jnp
from jax import lax
from jax.experimental import pallas as pl
from jax.experimental.pallas import tpu as pltpu
from jax.sharding import PartitionSpec as P

PARTS = (96, 88, 56, 16)
PIECES = len(PARTS)
STARTS = tuple(sum(PARTS[:p]) for p in range(PIECES))
MESH = pl.DeviceIdType.MESH


def bands(rows, extent):
    taps = rows.shape[-1]
    offset = jnp.arange(extent)[None, :] - jnp.arange(extent)[:, None] + taps // 2
    chosen = (offset[:, :, None] == jnp.arange(taps)[None, None, :]).astype(jnp.float32)
    return jnp.sum(chosen * rows, axis=-1)


def split(value):
    high = value.astype(jnp.bfloat16)
    low = (value - high.astype(jnp.float32)).astype(jnp.bfloat16)
    return high, low


def matmul(a, b):
    dot = functools.partial(jnp.dot, preferred_element_type=jnp.float32)
    return dot(a[0], b[0]) + (dot(a[0], b[1]) + dot(a[1], b[0]))


def kernel(
    views, owners, slots,
    outgoing, slot_weight, slot, planes, lines, seen, current, own_weight, out, weight_out, *scratch,
):
    sends, arrived, regroup = scratch[:PIECES], scratch[PIECES : 2 * PIECES], scratch[2 * PIECES : 3 * PIECES]
    (ratio_in, blurred, total, plane_all, line_all, plane_high, plane_low, line_high, line_low,
     z_send, z_recv, xy_send, xy_recv, m_send, m_recv, g_send, g_recv, own_sem,
     weight_all, w_send, w_recv, v_send, v_recv, w_sem) = scratch[3 * PIECES :]
    share, rows, lanes = current.shape
    here, view = lax.axis_index("joined"), lax.axis_index("view")
    owner_at = lambda d: lax.rem(here + d, owners)
    view_at = lambda u: lax.rem(view + u, views)
    sides = (view + 1 - 2 * lax.rem(view, 2), lax.rem(view + 2, 4))

    barrier = pltpu.get_barrier_semaphore()
    for d in range(1, owners):
        pl.semaphore_signal(barrier, inc=1, device_id={"joined": owner_at(d)}, device_id_type=MESH)
    for u in range(1, views):
        pl.semaphore_signal(barrier, inc=1, device_id={"view": view_at(u)}, device_id_type=MESH)
    pl.semaphore_wait(barrier, owners + views - 2)

    def matrix_copies(u):
        return [
            pltpu.make_async_remote_copy(
                src_ref=src, dst_ref=dst.at[view],
                send_sem=m_send.at[i, u - 1], recv_sem=m_recv.at[i, u - 1],
                device_id={"view": view_at(u)}, device_id_type=MESH,
            )
            for i, (src, dst) in enumerate(((planes, plane_all), (lines, line_all)))
        ]

    def z_copy(p, d):
        return pltpu.make_async_remote_copy(
            src_ref=sends[p].at[d - 1],
            dst_ref=arrived[p].at[pl.ds(here * slots, slots)],
            send_sem=z_send.at[p, d - 1], recv_sem=z_recv.at[p, d - 1],
            device_id={"joined": owner_at(d)}, device_id_type=MESH,
        )

    def xy_copy(p, u):
        return pltpu.make_async_remote_copy(
            src_ref=regroup[p].at[u - 1],
            dst_ref=ratio_in.at[view, :, pl.ds(STARTS[p], PARTS[p])],
            send_sem=xy_send.at[p, u - 1], recv_sem=xy_recv.at[p, u - 1],
            device_id={"view": view_at(u)}, device_id_type=MESH,
        )

    def gather_copy(k, side):
        return pltpu.make_async_remote_copy(
            src_ref=total.at[k], dst_ref=out.at[view, k],
            send_sem=g_send.at[k, side], recv_sem=g_recv.at[k, side],
            device_id={"view": sides[side]}, device_id_type=MESH,
        )

    def forward_copy(k, side):
        place = out.at[sides[side], k]
        return pltpu.make_async_remote_copy(
            src_ref=place, dst_ref=place,
            send_sem=g_send.at[k, 2], recv_sem=g_recv.at[k, 2],
            device_id={"view": sides[1 - side]}, device_id_type=MESH,
        )

    def weight_copy(d):
        return pltpu.make_async_remote_copy(
            src_ref=own_weight, dst_ref=weight_all.at[here],
            send_sem=w_send.at[d - 1], recv_sem=w_recv.at[d - 1],
            device_id={"joined": owner_at(d)}, device_id_type=MESH,
        )

    def weights_copy(u):
        return pltpu.make_async_remote_copy(
            src_ref=weight_all, dst_ref=weight_out.at[view],
            send_sem=v_send.at[u - 1], recv_sem=v_recv.at[u - 1],
            device_id={"view": view_at(u)}, device_id_type=MESH,
        )

    def own_copy(k):
        return pltpu.make_async_copy(total.at[k], out.at[view, k], own_sem.at[k])

    def pack(p):
        window = pl.ds(STARTS[p], PARTS[p])
        for d in list(range(1, owners)) + [0]:

            def fill(s, carry):
                at = owner_at(d) * slots + s
                piece = seen[outgoing[at], window] * slot_weight[at]
                if d == 0:
                    arrived[p][here * slots + s] = piece
                else:
                    sends[p][d - 1, s] = piece
                return carry

            lax.fori_loop(0, slots, fill, 0)
            if d:
                z_copy(p, d).start()

    def regroup_piece(p):
        for d in range(1, owners):
            z_copy(p, d).wait_recv()
        for u in list(range(1, views)) + [0]:

            def move(k, carry):
                piece = arrived[p][slot[view_at(u) * share + k]]
                if u == 0:
                    ratio_in[view, k, pl.ds(STARTS[p], PARTS[p])] = piece
                else:
                    regroup[p][u - 1, k] = piece
                return carry

            lax.fori_loop(0, share, move, 0)
            if u:
                xy_copy(p, u).start()

    own_weights = pltpu.make_async_copy(weight_all, weight_out.at[view], w_sem)
    pack(0)
    weight_all[here] = own_weight[...]
    for d in range(1, owners):
        weight_copy(d).start()
    plane_all[view] = planes[...]
    line_all[view] = lines[...]
    for u in range(1, views):
        for copy in matrix_copies(u):
            copy.start()
    pack(1)
    for u in range(1, views):
        for copy in matrix_copies(u):
            copy.wait_recv()

    def prepare(v, carry):
        for i in range(2):
            plane_high[v, i], plane_low[v, i] = split(plane_all[v, i])
            line_high[v, i], line_low[v, i] = split(line_all[v, i])

        def blur_one(k, inner):
            half = matmul(split(current[k]), (line_high[v, 1], line_low[v, 1]))
            blurred[v, k] = matmul((plane_high[v, 0], plane_low[v, 0]), split(half))
            return inner

        return lax.fori_loop(0, share, blur_one, carry)

    lax.fori_loop(0, views, prepare, 0)

    for p in range(PIECES):
        regroup_piece(p)
        if p == 0:
            for d in range(1, owners):
                weight_copy(d).wait_recv()
            for u in range(1, views):
                weights_copy(u).start()
            own_weights.start()
        if p + 2 < PIECES:
            pack(p + 2)
    for p in range(PIECES):
        for u in range(1, views):
            xy_copy(p, u).wait_recv()

    def finish_one(k):
        def back(v, inner):
            ratio = ratio_in[v, k] / blurred[v, k]
            half = matmul(split(ratio), (line_high[v, 0], line_low[v, 0]))
            return inner + matmul((plane_high[v, 1], plane_low[v, 1]), split(half))

        total[k] = lax.fori_loop(
            0, views, back, jnp.zeros((rows, lanes), jnp.float32), unroll=True
        )
        for side in range(2):
            gather_copy(k, side).start()
        own_copy(k).start()

    def forward_pair(pair):
        for side in range(2):
            gather_copy(2 * pair + side, side).wait_recv()
            forward_copy(2 * pair + side, side).start()

    def finish(pair, carry):
        finish_one(2 * pair)
        finish_one(2 * pair + 1)

        @pl.when(pair > 0)
        def _():
            forward_pair(pair - 1)

        return carry

    lax.fori_loop(0, share // 2, finish, 0)
    forward_pair(share // 2 - 1)

    for u in range(1, views):
        for copy in matrix_copies(u):
            copy.wait_send()
    for p in range(PIECES):
        for d in range(1, owners):
            z_copy(p, d).wait_send()
        for u in range(1, views):
            xy_copy(p, u).wait_send()

    for d in range(1, owners):
        weight_copy(d).wait_send()
    for u in range(1, views):
        weights_copy(u).wait()
    own_weights.wait()

    def drain(pair, carry):
        for side in range(2):
            k = 2 * pair + side
            own_copy(k).wait()
            gather_copy(k, side).wait_send()
            gather_copy(k, 1 - side).wait()
            forward_copy(k, side).wait()
        return carry

    lax.fori_loop(0, share // 2, drain, 0)


def exchange(views, owners, slots, outgoing, slot_weight, slot, planes, lines, seen, current, weight):
    share, rows, lanes = current.shape
    f32, bf16 = jnp.float32, jnp.bfloat16
    dma = pltpu.SemaphoreType.DMA
    smem, vmem = pl.BlockSpec(memory_space=pltpu.SMEM), pl.BlockSpec(memory_space=pltpu.VMEM)
    scratch = (
        [pltpu.VMEM((owners - 1, slots, part, lanes), f32) for part in PARTS]
        + [pltpu.VMEM((owners * slots, part, lanes), f32) for part in PARTS]
        + [pltpu.VMEM((views - 1, share, part, lanes), f32) for part in PARTS]
        + [pltpu.VMEM((views, share, rows, lanes), f32)] * 2
        + [pltpu.VMEM((share, rows, lanes), f32)]
        + [pltpu.VMEM((views,) + planes.shape, f32), pltpu.VMEM((views,) + lines.shape, f32)]
        + [pltpu.VMEM((views,) + planes.shape, bf16)] * 2
        + [pltpu.VMEM((views,) + lines.shape, bf16)] * 2
        + [dma((PIECES, owners - 1))] * 2
        + [dma((PIECES, views - 1))] * 2
        + [dma((2, views - 1))] * 2
        + [dma((share, 3))] * 2
        + [dma((share,))]
        + [pltpu.VMEM((owners,) + weight.shape, f32)]
        + [dma((owners - 1,))] * 2
        + [dma((views - 1,))] * 2
        + [dma(())]
    )
    return pl.pallas_call(
        functools.partial(kernel, views, owners, slots),
        out_shape=(
            jax.ShapeDtypeStruct((views, share, rows, lanes), f32),
            jax.ShapeDtypeStruct((views, owners) + weight.shape, f32),
        ),
        in_specs=[smem] * 3 + [vmem] * 5,
        out_specs=[pl.BlockSpec(memory_space=pl.ANY)] * 2,
        scratch_shapes=scratch,
        compiler_params=pltpu.CompilerParams(
            collective_id=0, has_side_effects=True, vmem_limit_bytes=56 * 1024 * 1024
        ),
        cost_estimate=pl.CostEstimate(
            flops=6 * 2 * views * share * 2 * rows * lanes * (rows + lanes) // 2,
            bytes_accessed=4 * (seen.size + 5 * current.size),
            transcendentals=0,
        ),
    )(outgoing, slot_weight, slot, planes, lines, seen, current, weight)


def shards(observed, estimate, psf_taps, tile_block, weight_level):
    owners, views = lax.axis_size("joined"), lax.axis_size("view")
    view_here, joined_here = lax.axis_index("view"), lax.axis_index("joined")
    tiles_dev, size_z, size_y, size_x = estimate.shape
    rows = size_z * size_y
    slots = 2 * tiles_dev // owners
    all_slots = owners * slots
    share = tiles_dev // views

    kernel_rows = psf_taps[0] / jnp.sum(psf_taps[0], axis=-1, keepdims=True)
    along_z = bands(kernel_rows[0], size_z)
    along_y = bands(kernel_rows[1], size_y)
    line = bands(kernel_rows[2], size_x)
    plane = (along_z[:, None, :, None] * along_y[None, :, None, :]).reshape(rows, rows)

    listing = lax.dynamic_index_in_dim(tile_block, view_here, 0, keepdims=False)
    owner_of = (listing // tiles_dev).reshape(owners, tiles_dev)
    earlier = jnp.arange(tiles_dev)[None, :] < jnp.arange(tiles_dev)[:, None]
    matching = owner_of[:, :, None] == owner_of[:, None, :]
    rank = jnp.sum((matching & earlier[None]).astype(jnp.int32), axis=2)
    source = jnp.arange(owners, dtype=jnp.int32)[:, None]
    arrive = (source * slots + rank).reshape(-1)
    here = lax.dynamic_slice_in_dim(owner_of * slots + rank, joined_here, 1, 0)[0]
    fills = (here[None, :] == jnp.arange(all_slots)[:, None]).astype(jnp.int32)
    outgoing = jnp.sum(fills * jnp.arange(tiles_dev, dtype=jnp.int32)[None, :], axis=1)
    local = jnp.arange(tiles_dev, dtype=jnp.int32) + joined_here * tiles_dev
    hits = (tile_block[:, None, :] == local[None, :, None]).astype(jnp.int32)
    hits_here = lax.dynamic_index_in_dim(hits, view_here, 0, keepdims=False)
    slot = jnp.sum(hits_here * arrive[None, :], axis=1)

    tile_weight = (weight_level[0].astype(jnp.float32) + 1.0) / 8.0
    slot_weight = jnp.sum(fills.astype(jnp.float32) * tile_weight[None, :], axis=1)
    current = estimate.reshape(tiles_dev, rows, size_x)
    mine = lax.dynamic_slice_in_dim(current, view_here * share, share, 0)
    weight_row = jnp.broadcast_to(jnp.pad(tile_weight, (0, -tiles_dev % 128)), (8, 128))
    numerator, all_weight = exchange(
        views, owners, slots,
        outgoing, slot_weight, slot,
        jnp.stack([plane, plane.T]), jnp.stack([line, line.T]),
        observed.reshape(tiles_dev, rows, size_x), mine, weight_row,
    )
    numerator = numerator.reshape(tiles_dev, rows, size_x)
    all_weight = all_weight[:, :, 0, :tiles_dev].reshape(views, 1, -1)
    denominator = jnp.sum(hits.astype(jnp.float32) * all_weight, axis=(0, 2))
    refined = current * (numerator / denominator[:, None, None])
    return refined.reshape(estimate.shape)


def solution(mesh):
    return jax.shard_map(
        shards,
        mesh=mesh,
        in_specs=(
            P("view", "joined", None, None, None),
            P("joined", None, None, None),
            P("view", None, None),
            P(),
            P("view", "joined"),
        ),
        out_specs=P("joined", None, None, None),
        check_vma=False,
    )
```
